1024 devices in a mesh: dp: 16 (over z), expert: 64 (over x, y, core).
Axes of the slice: x: 4, y: 8, z: 16, core: 2. Of those that a mesh axis runs over, the one named last changes fastest.
Arguments:
- tokens: bfloat16 [1024, 3584], P(('dp', 'expert')), may hold values from -6 to 6
- expert_ids: int32 [1024, 8], P('dp'), may hold values from 0 to 63, as said below
- gates: bfloat16 [1024, 8], P('dp'), may hold values from 0.099609375 to 1
- w_gate: bfloat16 [64, 3584, 2048], P('expert', None, 'dp'), may hold values from -0.09375 to 0.09375
- w_up: bfloat16 [64, 3584, 2048], P('expert', None, 'dp'), may hold values from -0.09375 to 0.09375
- w_down: bfloat16 [64, 2048, 3584], P('expert', 'dp'), may hold values from -0.125 to 0.125
- cotangent: bfloat16 [1024, 3584], P(('dp', 'expert')), may hold values from -6 to 6
Outputs:
- mixed: bfloat16 [1024, 3584], P(('dp', 'expert'))
- grad_tokens: bfloat16 [1024, 3584], P(('dp', 'expert'))
- grad_gates: float32 [1024, 8], P(('dp', 'expert'))
The draws below stay inside these ranges and needn't reach their ends.
Inputs may be any that keep to these rules, and one draw needn't show every extreme that they name: `expert_ids`: each row names 8 distinct experts, exactly two from each of four of the 8 groups of 8 consecutive experts. In each aligned block of 64 rows no expert is named by more than 9 rows, and some expert by exactly 9.
All inputs are finite; a program needn't handle non-finite values.
Results may differ from the reference program's by a relative error of at most 0.035.
Values may be sent and summed in bfloat16 or wider, within the bound.
No kernel may reach another device: no remote copies, remote signals or barrier semaphores. Data moves between devices by JAX's collectives and lax.ppermute only.
A program may use at most 32 MiB of HBM per device.

```python
import math
import jax
import jax.numpy as jnp
from jax import lax

D = 3584
FF = 2048
TOPK = 8
EXPERTS = 64
GROUP = 8
HB = 128
ROW_TOKENS = 64
TOKENS = 1024
CAP = 9
N_DP = 16


def route_block(key):
    key_hot, key_cold, key_rank, key_inner = jax.random.split(key, 4)
    hot_node = jax.random.randint(key_hot, (), 0, 8).astype(jnp.int32)
    node_ids = jnp.arange(8, dtype=jnp.int32)
    cold_score = jax.random.randint(key_cold, (8,), 0, 1 << 20).astype(jnp.int32) * 8 + node_ids
    cold_score = jnp.where(node_ids == hot_node, jnp.int32(1 << 30), cold_score)
    cold_nodes = jnp.argsort(cold_score)[:7].astype(jnp.int32)
    token_ids = jnp.arange(ROW_TOKENS, dtype=jnp.int32)
    rank_score = jax.random.randint(key_rank, (ROW_TOKENS,), 0, 1 << 20).astype(jnp.int32) * ROW_TOKENS + token_ids
    token_rank = jnp.argsort(jnp.argsort(rank_score)).astype(jnp.int32)
    hot_count = (CAP - 1) * GROUP // 2 + 1
    with_hot = token_rank < hot_count
    column = jnp.arange(4, dtype=jnp.int32)
    place_hot = (3 * token_rank[:, None] + column) % 7
    place_cold = (4 * (token_rank[:, None] - hot_count) + column) % 7
    picked = cold_nodes[jnp.where(with_hot[:, None], place_hot, place_cold)]
    chosen_nodes = jnp.where(with_hot[:, None] & (column == 3)[None, :], hot_node, picked).astype(jnp.int32)
    member = jnp.sum((chosen_nodes[:, :, None] == node_ids).astype(jnp.int32), axis=1)
    position = jnp.cumsum(member, axis=0) - 1
    node_position = jnp.take_along_axis(position, chosen_nodes, axis=1)
    inner_score = jax.random.randint(key_inner, (8, GROUP), 0, 1 << 20).astype(jnp.int32) * GROUP + jnp.arange(GROUP, dtype=jnp.int32)
    order_in_node = jnp.argsort(inner_score, axis=1).astype(jnp.int32)
    first_pick = order_in_node[chosen_nodes, 2 * node_position % GROUP]
    second_pick = order_in_node[chosen_nodes, (2 * node_position + 1) % GROUP]
    chosen = jnp.stack([first_pick, second_pick], axis=2) + chosen_nodes[:, :, None] * GROUP
    return chosen.reshape(ROW_TOKENS, TOPK).astype(jnp.int32)


def draw_expert_ids(key, part):
    key = jax.random.fold_in(key, 11)
    block_keys = jax.random.split(key, TOKENS // ROW_TOKENS)
    return jax.vmap(route_block)(block_keys).reshape(TOKENS, TOPK).astype(jnp.int32)


def levels(stream_key, extent, cuts, smallest, high):
    level, own = 1.0, jax.random.fold_in(stream_key, 6)
    for axis_at, shards_of in cuts:
        draws = jnp.exp(jax.random.uniform(jax.random.fold_in(own, axis_at), (shards_of,), jnp.float32, smallest / len(cuts), high / len(cuts)))
        level = level * jnp.repeat(draws, extent[axis_at] // shards_of).reshape([-1 if axis == axis_at else 1 for axis in range(len(extent))])
    return level


def gaussian(stream_key, dims, deviation, limit, pieces=(), held_as=jnp.bfloat16):
    loudness = levels(stream_key, dims, pieces, -0.22, 0.18) if pieces else 1.0
    drawn = jax.random.normal(stream_key, dims, jnp.float32) * deviation * loudness
    return jnp.minimum(jnp.maximum(drawn, -limit), limit).astype(held_as)


def setup_inputs(seed: int = 0) -> dict:
    keys = jax.random.split(jax.random.key(seed), 8)
    return {
        "tokens": gaussian(keys[0], (TOKENS, D), 1.0, 6.0, ((0, 1024),)),
        "expert_ids": draw_expert_ids(jax.random.fold_in(keys[7], 71), 0),
        "gates": jnp.clip(jnp.exp(math.log(1.0) - 2.306499 * jax.random.uniform(keys[2], (TOKENS, TOPK), jnp.float32) ** levels(keys[2], (TOKENS, TOPK), ((0, 16),), -0.2, 0.2)), 0.099609375, 1.0).astype(jnp.bfloat16),
        "w_gate": gaussian(keys[3], (EXPERTS, D, FF), D ** -0.5, 0.09375, ((0, 64), (2, 16))),
        "w_up": gaussian(keys[4], (EXPERTS, D, FF), D ** -0.5, 0.09375, ((0, 64), (2, 16))),
        "w_down": gaussian(keys[5], (EXPERTS, FF, D), FF ** -0.5, 0.125, ((0, 64), (1, 16))),
        "cotangent": gaussian(keys[6], (TOKENS, D), 1.0, 6.0, ((0, 1024),)),
    }


def reference(tokens, expert_ids, gates, w_gate, w_up, w_down, cotangent):
    routes = expert_ids.reshape(N_DP, ROW_TOKENS, TOPK)
    onehot = (routes[..., None] == jnp.arange(EXPERTS, dtype=jnp.int32)).astype(jnp.float32)
    member = jnp.sum(onehot, axis=2)
    slot_index = jnp.cumsum(member, axis=1) - 1.0
    slot_range = jnp.arange(CAP).astype(jnp.float32)
    chooser = member[..., None] * (slot_index[..., None] == slot_range).astype(jnp.float32)
    gate_vals = gates.astype(jnp.float32).reshape(N_DP, ROW_TOKENS, TOPK)
    gate_sel = jnp.einsum('nbke,nbk->nbe', onehot, gate_vals)
    token_vals = tokens.astype(jnp.float32).reshape(N_DP, ROW_TOKENS, D)
    cot_vals = cotangent.astype(jnp.float32).reshape(N_DP, ROW_TOKENS, D)
    expert_input = jnp.einsum('nbec,nbd->encd', chooser, token_vals).astype(jnp.bfloat16)
    cot_rows = jnp.einsum('nbec,nbd->encd', chooser, cot_vals)
    gate_rows = jnp.einsum('nbec,nbe->enc', chooser, gate_sel)
    grad_rows = (cot_rows * gate_rows[..., None]).astype(jnp.bfloat16)
    row_count = N_DP * CAP

    def expert_step(operands):
        inputs, grads_in, gate_mat, up_mat, down_mat = operands
        gate_pre = jnp.dot(inputs, gate_mat, preferred_element_type=jnp.float32)
        up_pre = jnp.dot(inputs, up_mat, preferred_element_type=jnp.float32)
        sig_gate = jax.nn.sigmoid(gate_pre)
        activated = (gate_pre * sig_gate * up_pre).astype(jnp.bfloat16)
        act_blocks = activated.astype(jnp.float32).reshape(row_count, N_DP, HB)
        down_blocks = down_mat.astype(jnp.float32).reshape(N_DP, HB, D)
        partial_value = jnp.einsum('rbh,bhd->brd', act_blocks, down_blocks).astype(jnp.bfloat16)
        partial_value = lax.optimization_barrier(partial_value)
        expert_out = jnp.sum(partial_value.astype(jnp.float32), axis=0).astype(jnp.bfloat16)
        grad_hid = jnp.dot(grads_in, down_mat.T, preferred_element_type=jnp.float32)
        grad_gate = (grad_hid * up_pre * sig_gate * (1.0 + gate_pre * (1.0 - sig_gate))).astype(jnp.bfloat16)
        grad_up = (grad_hid * gate_pre * sig_gate).astype(jnp.bfloat16)
        gate_cols = gate_mat.astype(jnp.float32).reshape(D, N_DP, HB)
        up_cols = up_mat.astype(jnp.float32).reshape(D, N_DP, HB)
        back = jnp.einsum('rbh,dbh->brd', grad_gate.astype(jnp.float32).reshape(row_count, N_DP, HB), gate_cols)
        back = back + jnp.einsum('rbh,dbh->brd', grad_up.astype(jnp.float32).reshape(row_count, N_DP, HB), up_cols)
        back = lax.optimization_barrier(back.astype(jnp.bfloat16))
        grad_input = jnp.sum(back.astype(jnp.float32), axis=0).astype(jnp.bfloat16)
        return expert_out, grad_input

    outputs, input_grads = lax.map(expert_step, (expert_input.reshape(EXPERTS, row_count, D), grad_rows.reshape(EXPERTS, row_count, D), w_gate, w_up, w_down))
    out_vals = outputs.astype(jnp.float32).reshape(EXPERTS, N_DP, CAP, D)
    weighted = chooser * gate_sel[..., None]
    mixed = jnp.einsum('nbec,encd->nbd', weighted, out_vals).reshape(TOKENS, D).astype(jnp.bfloat16)
    slot_dots = jnp.einsum('encd,encd->enc', out_vals, cot_rows)
    route_grad = jnp.einsum('nbec,enc->nbe', chooser, slot_dots)
    grad_gates = jnp.einsum('nbke,nbe->nbk', onehot, route_grad).reshape(TOKENS, TOPK)
    grad_vals = input_grads.astype(jnp.float32).reshape(EXPERTS, N_DP, CAP, D)
    grad_tokens = jnp.einsum('nbec,encd->nbd', chooser, grad_vals).reshape(TOKENS, D).astype(jnp.bfloat16)
    return mixed, grad_tokens, grad_gates
```

```python
import jax
import jax.numpy as jnp
import numpy as np
from jax import lax
from jax.sharding import Mesh, PartitionSpec as P

F32 = jnp.float32
BF16 = jnp.bfloat16
CAP = 9
QN = 4
PIECES = 2 * QN
PACK = PIECES * CAP
ZA, ZC = 4, 4
EXTRA = 128
ZAXES = ("za", "zc")
PLANE = ("x", "y")


def shift_z(values, step):
    n = ZA * ZC
    return lax.ppermute(values, ZAXES, [(i, (i + step) % n) for i in range(n)])


def swap_core(values):
    return lax.ppermute(values, "c", [(0, 1), (1, 0)])


def unpack_matrix():
    rows = np.arange(ZA * PACK)
    slot = rows % CAP
    chunk = rows // CAP % ZA
    half = rows // (CAP * ZA) % 2
    piece = rows // (CAP * ZA * 2)
    source = ((chunk * 2 + half) * QN + piece) * CAP + slot
    matrix = np.zeros((ZA * PACK, ZA * PACK), np.float32)
    matrix[rows, source] = 1
    return matrix


def dot(a, b, dims=((1,), (0,))):
    return lax.dot_general(a, b, (dims, ((), ())), preferred_element_type=F32)


def local(tokens, expert_ids, gates, w_gate, w_up, w_down, cotangent):
    width = tokens.shape[1]
    lanes = width // QN
    half_width = width // 2
    chips = lax.axis_size(PLANE)
    block = expert_ids.shape[0]
    topk = expert_ids.shape[1]
    core = lax.axis_index("c").astype(jnp.int32)
    expert = lax.axis_index(PLANE).astype(jnp.int32) * 2 + core
    sibling = expert + 1 - 2 * core
    w_gate, w_up, w_down = w_gate[0], w_up[0], w_down[0]

    payload = jnp.concatenate(
        [tokens.reshape(QN, lanes), cotangent.reshape(QN, lanes)], axis=0
    )
    spread = jnp.broadcast_to(payload[None], (chips, PIECES, lanes))
    gathered = lax.all_to_all(spread, PLANE, 0, 0, tiled=True).reshape(chips * PIECES, lanes)

    ids = expert_ids.T
    named = ids == expert
    member = jnp.stack([jnp.any(named, axis=0), jnp.any(ids == sibling, axis=0)])
    token_row = lax.broadcasted_iota(jnp.int32, (block, block), 0)
    token_col = lax.broadcasted_iota(jnp.int32, (block, block), 1)
    earlier = (token_row < token_col).astype(BF16)
    before = dot(member.astype(BF16), earlier)
    place = jnp.where(member, before + 1.0, 0.0)
    spot = lax.broadcasted_iota(jnp.int32, (block, chips * PIECES), 1)
    token_at = lax.broadcasted_iota(jnp.int32, (block, chips * PIECES), 0)
    expand = (token_at == 2 * (spot // PIECES) + core).astype(BF16)
    place_cols = dot(place.astype(BF16), expand)
    row = lax.broadcasted_iota(jnp.int32, (2 * PACK, chips * PIECES), 0)
    col = lax.broadcasted_iota(jnp.int32, (2 * PACK, chips * PIECES), 1)
    held = jnp.where(row < PACK, place_cols[0:1], place_cols[1:2])
    choose = (
        (held == (row % CAP + 1).astype(F32)) & (row // CAP % PIECES == col % PIECES)
    ).astype(BF16)

    gate_of = jnp.sum(jnp.where(named, gates.T.astype(F32), 0.0), axis=0)
    slot_row = lax.broadcasted_iota(jnp.int32, (PACK, block), 0) % CAP + 1
    in_slot = place[0:1] == slot_row.astype(F32)
    gate_rows = jnp.sum(jnp.where(in_slot, gate_of[None], 0.0), axis=1, keepdims=True)
    route_rows = dot(in_slot[:CAP].astype(BF16), named.astype(BF16), ((1,), (1,)))

    chosen = dot(choose, gathered).astype(BF16)
    packed = chosen[:PACK] + swap_core(chosen[PACK:])

    turn = jnp.asarray(unpack_matrix(), BF16)
    strided = lax.all_gather(packed, "za", axis=0).reshape(ZA * PACK, lanes)
    turned = dot(turn, strided).astype(BF16)
    group = turned.shape[0] // QN
    here = jnp.concatenate([turned[q * group : (q + 1) * group] for q in range(QN)], axis=1)
    below = shift_z(here, 1)
    above = shift_z(here, -1)
    far_left = shift_z(below[:, :half_width], 1)
    far_right = shift_z(above[:, half_width:], -1)
    far = jnp.concatenate([far_left, far_right], axis=1)
    rows = group // 2

    def expert_terms(values):
        gate_pre = dot(values, w_gate)[:rows]
        up_pre = dot(values, w_up)[:rows]
        grad_hid = dot(values, w_down, ((1,), (1,)))[rows:]
        sig = jax.nn.sigmoid(gate_pre)
        hid = (gate_pre * sig * up_pre).astype(BF16)
        grad_gate = (grad_hid * up_pre * sig * (1.0 + gate_pre * (1.0 - sig))).astype(BF16)
        grad_up = (grad_hid * gate_pre * sig).astype(BF16)
        none = jnp.zeros_like(hid)
        out = dot(jnp.concatenate([hid, none], axis=0), w_down)
        out = out + dot(jnp.concatenate([none, grad_gate], axis=0), w_gate, ((1,), (1,)))
        out = out + dot(jnp.concatenate([none, grad_up], axis=0), w_up, ((1,), (1,)))
        return out.astype(BF16)

    terms_far = expert_terms(far)
    terms_here, terms_below, terms_above = (
        expert_terms(here),
        expert_terms(below),
        expert_terms(above),
    )

    back_left = shift_z(terms_far[:, :half_width], -1)
    back_right = shift_z(terms_far[:, half_width:], 1)
    low = jnp.concatenate(
        [
            (terms_below[:, :half_width].astype(F32) + back_left.astype(F32)).astype(BF16),
            terms_below[:, half_width:],
        ],
        axis=1,
    )
    high = jnp.concatenate(
        [
            terms_above[:, :half_width],
            (terms_above[:, half_width:].astype(F32) + back_right.astype(F32)).astype(BF16),
        ],
        axis=1,
    )
    from_above = shift_z(low, -1)
    from_below = shift_z(high, 1)
    summed = (
        terms_here.astype(F32) + from_above.astype(F32) + from_below.astype(F32)
    ).astype(BF16)
    stacked = jnp.concatenate(
        [summed[:, q * lanes : (q + 1) * lanes] for q in range(QN)], axis=0
    )
    outgoing = dot(turn, stacked, ((0,), (0,))).astype(BF16).reshape(ZA, PACK, lanes)
    arrived = lax.all_to_all(outgoing, "za", 0, 0, tiled=True)
    results = jnp.sum(arrived.astype(F32), axis=0)

    half = PACK // 2
    value_rows = results[:half].astype(BF16).astype(F32)
    dots = jnp.sum(value_rows * packed[half:].astype(F32), axis=1)
    slot_dots = jnp.sum(dots.reshape(QN, CAP), axis=0)[:, None]
    dots_high = lax.reduce_precision(slot_dots, 8, 7)
    dots_low = slot_dots - dots_high
    carried = jnp.concatenate([dots_high * route_rows, dots_low * route_rows], axis=1)
    carried = jnp.pad(carried, ((0, PACK - CAP), (0, EXTRA - 2 * topk)))
    scaled = jnp.concatenate([results * gate_rows, carried], axis=1).astype(BF16)
    both = jnp.concatenate([scaled, swap_core(scaled)], axis=0)

    dense = dot(choose, both, ((0,), (0,))).astype(BF16)
    dense = dense.reshape(chips, PIECES, lanes + EXTRA)
    mine = lax.all_to_all(dense, PLANE, 0, 0, tiled=True)
    total = jnp.sum(mine.astype(F32), axis=0)
    mixed = total[:QN, :lanes].astype(BF16).reshape(1, width)
    grad_tokens = total[QN:, :lanes].astype(BF16).reshape(1, width)
    grad_gates = total[0:1, lanes : lanes + topk] + total[0:1, lanes + topk : lanes + 2 * topk]
    return mixed, grad_tokens, grad_gates


def solution(mesh, plane=(4, 8, 2)):
    fine = Mesh(mesh.devices.reshape((ZA, ZC) + plane), ZAXES + PLANE + ("c",))
    rows = P(ZAXES + PLANE + ("c",), None)
    experts = PLANE + ("c",)
    return jax.shard_map(
        local,
        mesh=fine,
        in_specs=(
            rows,
            P(ZAXES, None),
            P(ZAXES, None),
            P(experts, None, ZAXES),
            P(experts, None, ZAXES),
            P(experts, ZAXES, None),
            rows,
        ),
        out_specs=(rows, rows, rows),
        check_vma=False,
    )
```

```python
import jax
import jax.numpy as jnp
import numpy as np
from jax import lax
from jax.experimental import pallas as pl
from jax.sharding import Mesh, PartitionSpec as P

F32 = jnp.float32
BF16 = jnp.bfloat16
CAP = 9
QN = 4
PIECES = 2 * QN
PACK = PIECES * CAP
ZA, ZB, ZD = 4, 2, 2
EXTRA = 128
ZAXES = ("za", "zb", "zd")
PLANE = ("x", "y")


def shift_z(values, step):
    n = ZA * ZB * ZD
    return lax.ppermute(values, ZAXES, [(i, (i + step) % n) for i in range(n)])


def swap_core(values):
    return lax.ppermute(values, "c", [(0, 1), (1, 0)])


def turn_matrices():
    rows = np.arange(ZB * ZA * PACK)
    slot = rows % CAP
    za = rows // CAP % ZA
    half = rows // (CAP * ZA) % 2
    kind = rows // (CAP * ZA * 2) % ZB
    piece = rows // (CAP * ZA * 2 * ZB)
    matrix = np.zeros((2, ZB * ZA * PACK, ZB * ZA * PACK), np.float32)
    for last in range(2):
        zb = np.where(kind == 1, last, 1 - last)
        source = (((za * ZB + zb) * 2 + half) * QN + piece) * CAP + slot
        matrix[last, rows, source] = 1
    return matrix


def dot(a, b, dims=((1,), (0,))):
    return lax.dot_general(a, b, (dims, ((), ())), preferred_element_type=F32)


def spread_kernel(tokens, cotangent, out):
    lanes = out.shape[2]
    rows = [
        ref[:, q * lanes : (q + 1) * lanes] for ref in (tokens, cotangent) for q in range(QN)
    ]
    out[...] = jnp.broadcast_to(jnp.concatenate(rows, axis=0)[None], out.shape)


def pack_kernel(here, above, below, out):
    lanes = out.shape[1]
    group = here.shape[0]
    row = lax.broadcasted_iota(jnp.int32, (ZA * PACK, group), 0)
    col = lax.broadcasted_iota(jnp.int32, (ZA * PACK, group), 1)
    source = (row // (QN * CAP) % 2 * ZA + row // PACK) * CAP + row % CAP
    total = jnp.zeros(out.shape, F32)
    for q in range(QN):
        cols = slice(q * lanes, (q + 1) * lanes)
        summed = here[:, cols].astype(F32) + above[:, cols].astype(F32)
        summed = (summed + below[:, cols].astype(F32)).astype(BF16)
        pick = ((source == col) & (row // CAP % QN == q)).astype(F32).astype(BF16)
        total = total + dot(pick, summed)
    out[...] = total.astype(BF16)


def finish_kernel(mine, mixed, grad_tokens, grad_gates):
    lanes = mixed.shape[1] // QN
    topk = grad_gates.shape[1]
    total = mine[0].astype(F32)
    for chip in range(1, mine.shape[0]):
        total = total + mine[chip].astype(F32)
    for q in range(QN):
        cols = slice(q * lanes, (q + 1) * lanes)
        mixed[:, cols] = total[q : q + 1, :lanes].astype(BF16)
        grad_tokens[:, cols] = total[QN + q : QN + q + 1, :lanes].astype(BF16)
    grad_gates[...] = (
        total[0:1, lanes : lanes + topk] + total[0:1, lanes + topk : lanes + 2 * topk]
    )


def local(tokens, expert_ids, gates, w_gate, w_up, w_down, cotangent):
    width = tokens.shape[1]
    lanes = width // QN
    half_width = width // 2
    chips = lax.axis_size(PLANE)
    block = expert_ids.shape[0]
    topk = expert_ids.shape[1]
    core = lax.axis_index("c").astype(jnp.int32)
    expert = lax.axis_index(PLANE).astype(jnp.int32) * 2 + core
    sibling = expert + 1 - 2 * core
    w_gate, w_up, w_down = w_gate[0], w_up[0], w_down[0]

    spread = pl.pallas_call(
        spread_kernel, out_shape=jax.ShapeDtypeStruct((chips, PIECES, lanes), BF16)
    )(tokens, cotangent)
    gathered = lax.all_to_all(spread, PLANE, 0, 0, tiled=True).reshape(chips * PIECES, lanes)

    ids = expert_ids.T
    named = ids == expert
    member = jnp.stack([jnp.any(named, axis=0), jnp.any(ids == sibling, axis=0)])
    token_row = lax.broadcasted_iota(jnp.int32, (block, block), 0)
    token_col = lax.broadcasted_iota(jnp.int32, (block, block), 1)
    earlier = (token_row < token_col).astype(BF16)
    before = dot(member.astype(BF16), earlier)
    place = jnp.where(member, before + 1.0, 0.0)
    spot = lax.broadcasted_iota(jnp.int32, (block, chips * PIECES), 1)
    token_at = lax.broadcasted_iota(jnp.int32, (block, chips * PIECES), 0)
    expand = (token_at == 2 * (spot // PIECES) + core).astype(BF16)
    place_cols = dot(place.astype(BF16), expand)
    row = lax.broadcasted_iota(jnp.int32, (2 * PACK, chips * PIECES), 0)
    col = lax.broadcasted_iota(jnp.int32, (2 * PACK, chips * PIECES), 1)
    held = jnp.where(row < PACK, place_cols[0:1], place_cols[1:2])
    choose = (
        (held == (row % CAP + 1).astype(F32)) & (row // CAP % PIECES == col % PIECES)
    ).astype(BF16)

    gate_of = jnp.sum(jnp.where(named, gates.T.astype(F32), 0.0), axis=0)
    slot_row = lax.broadcasted_iota(jnp.int32, (PACK, block), 0) % CAP + 1
    in_slot = place[0:1] == slot_row.astype(F32)
    gate_rows = jnp.sum(jnp.where(in_slot, gate_of[None], 0.0), axis=1, keepdims=True)
    route_rows = dot(in_slot[:CAP].astype(BF16), named.astype(BF16), ((1,), (1,)))

    chosen = dot(choose, gathered).astype(BF16)
    packed = chosen[:PACK] + swap_core(chosen[PACK:])

    zb = lax.axis_index("zb").astype(jnp.int32)
    zd = lax.axis_index("zd").astype(jnp.int32)
    turns = jnp.asarray(turn_matrices(), BF16)
    turn_own = lax.dynamic_index_in_dim(turns, zb, 0, keepdims=False)
    turn_other = lax.dynamic_index_in_dim(turns, jnp.where(zd == 1, 1 - zb, zb), 0, keepdims=False)
    same = lax.all_gather(packed, ("za", "zb"), axis=0, tiled=True)
    middle = same.shape[0] // 2
    from_below = shift_z(same[:middle], 1)
    from_above = shift_z(same[middle:], -1)
    group = ZA * 2 * CAP

    def in_rows(turned):
        turned = turned.astype(BF16)
        return jnp.concatenate(
            [turned[2 * q * group : 2 * (q + 1) * group] for q in range(QN)], axis=1
        )

    def expert_terms(values):
        gate_pre = dot(values, w_gate).reshape(2, group, -1)[:, : group // 2]
        up_pre = dot(values, w_up).reshape(2, group, -1)[:, : group // 2]
        grad_hid = dot(values, w_down, ((1,), (1,))).reshape(2, group, -1)[:, group // 2 :]
        sig = jax.nn.sigmoid(gate_pre)
        hid = (gate_pre * sig * up_pre).astype(BF16)
        grad_gate = (grad_hid * up_pre * sig * (1.0 + gate_pre * (1.0 - sig))).astype(BF16)
        grad_up = (grad_hid * gate_pre * sig).astype(BF16)
        none = jnp.zeros_like(hid)

        def in_half(first, second):
            return jnp.concatenate([first, second], axis=1).reshape(2 * group, -1)

        out = dot(in_half(hid, none), w_down)
        out = out + dot(in_half(none, grad_gate), w_gate, ((1,), (1,)))
        out = out + dot(in_half(none, grad_up), w_up, ((1,), (1,)))
        return out.astype(BF16)

    terms_own = expert_terms(in_rows(dot(turn_own, same)))
    terms_far, terms_here = terms_own[:group], terms_own[group:]

    back_left = shift_z(terms_far[:, :half_width], -1)
    back_right = shift_z(terms_far[:, half_width:], 1)
    other = dot(turn_other[:, :middle], from_below) + dot(turn_other[:, middle:], from_above)
    terms_other = expert_terms(in_rows(other))
    terms_below, terms_above = terms_other[:group], terms_other[group:]
    low = jnp.concatenate(
        [
            (terms_below[:, :half_width].astype(F32) + back_left.astype(F32)).astype(BF16),
            terms_below[:, half_width:],
        ],
        axis=1,
    )
    high = jnp.concatenate(
        [
            terms_above[:, :half_width],
            (terms_above[:, half_width:].astype(F32) + back_right.astype(F32)).astype(BF16),
        ],
        axis=1,
    )
    outgoing = pl.pallas_call(
        pack_kernel, out_shape=jax.ShapeDtypeStruct((ZA * PACK, lanes), BF16)
    )(terms_here, shift_z(low, -1), shift_z(high, 1)).reshape(ZA, PACK, lanes)
    arrived = lax.all_to_all(outgoing, "za", 0, 0, tiled=True)
    results = jnp.sum(arrived.astype(F32), axis=0)

    half = PACK // 2
    value_rows = results[:half].astype(BF16).astype(F32)
    dots = jnp.sum(value_rows * packed[half:].astype(F32), axis=1)
    slot_dots = jnp.sum(dots.reshape(QN, CAP), axis=0)[:, None]
    dots_high = lax.reduce_precision(slot_dots, 8, 7)
    dots_low = slot_dots - dots_high
    carried = jnp.concatenate([dots_high * route_rows, dots_low * route_rows], axis=1)
    carried = jnp.pad(carried, ((0, PACK - CAP), (0, EXTRA - 2 * topk)))
    scaled = jnp.concatenate([results * gate_rows, carried], axis=1).astype(BF16)
    both = jnp.concatenate([scaled, swap_core(scaled)], axis=0)

    dense = dot(choose, both, ((0,), (0,))).astype(BF16)
    dense = dense.reshape(chips, PIECES, lanes + EXTRA)
    mine = lax.all_to_all(dense, PLANE, 0, 0, tiled=True)
    return pl.pallas_call(
        finish_kernel,
        out_shape=(
            jax.ShapeDtypeStruct((1, width), BF16),
            jax.ShapeDtypeStruct((1, width), BF16),
            jax.ShapeDtypeStruct((1, topk), F32),
        ),
    )(mine)


def solution(mesh, plane=(4, 8, 2)):
    fine = Mesh(mesh.devices.reshape((ZA, ZB, ZD) + plane), ZAXES + PLANE + ("c",))
    rows = P(ZAXES + PLANE + ("c",), None)
    experts = PLANE + ("c",)
    return jax.shard_map(
        local,
        mesh=fine,
        in_specs=(
            rows,
            P(ZAXES, None),
            P(ZAXES, None),
            P(experts, None, ZAXES),
            P(experts, None, ZAXES),
            P(experts, ZAXES, None),
            rows,
        ),
        out_specs=(rows, rows, rows),
        check_vma=False,
    )
```

```python
import jax
import jax.numpy as jnp
import numpy as np
from jax import lax
from jax.experimental import pallas as pl
from jax.experimental.pallas import tpu as pltpu
from jax.sharding import Mesh, PartitionSpec as P

F32 = jnp.float32
BF16 = jnp.bfloat16
CAP = 9
QN = 4
PIECES = 2 * QN
PACK = PIECES * CAP
ZA, ZB, ZD = 4, 2, 2
EXTRA = 128
ZAXES = ("za", "zb", "zd")
PLANE = ("x", "y")


def shift_z(values, step):
    n = ZA * ZB * ZD
    return lax.ppermute(values, ZAXES, [(i, (i + step) % n) for i in range(n)])


def both_cores(values):
    return lax.all_gather(values, "c", axis=0)


def dot(a, b, dims=((1,), (0,))):
    return lax.dot_general(a, b, (dims, ((), ())), preferred_element_type=F32)


def one_hot(mask):
    return mask.astype(F32).astype(BF16)


def vmem_call(body, out_shape, **kwargs):
    return pl.pallas_call(
        body,
        out_shape=out_shape,
        compiler_params=pltpu.CompilerParams(vmem_limit_bytes=16 * 2**20),
        **kwargs,
    )


def spread_kernel(tokens, cotangent, out):
    lanes = out.shape[2]
    rows = [
        ref[:, q * lanes : (q + 1) * lanes] for ref in (tokens, cotangent) for q in range(QN)
    ]
    out[...] = jnp.broadcast_to(jnp.concatenate(rows, axis=0)[None], out.shape)


def expert_kernel(base, low, high, w_gate, w_up, w_down, *outs):
    lanes = low.shape[1]
    middle = low.shape[0]
    count = base.shape[0]
    first, second = outs[: len(outs) // 2 + len(outs) % 2], outs[-(len(outs) // 2) :]
    spots = lax.broadcasted_iota(jnp.int32, (count, middle), 1)
    gate_pre = up_pre = grad_hid = jnp.zeros((count, w_down.shape[0]), F32)
    for q in range(QN):
        cols = slice(q * lanes, (q + 1) * lanes)
        rows = []
        for half in range(2):
            want = base[...] + (half * QN + q) * CAP
            part = dot(one_hot(spots == want), low[...])
            part = part + dot(one_hot(spots + middle == want), high[...])
            rows.append(part.astype(BF16))
        gate_pre = gate_pre + dot(rows[0], w_gate[cols, :])
        up_pre = up_pre + dot(rows[0], w_up[cols, :])
        grad_hid = grad_hid + dot(rows[1], w_down[:, cols], ((1,), (1,)))
    sig = 1.0 / (1.0 + jnp.exp(-gate_pre))
    hid = (gate_pre * sig * up_pre).astype(BF16)
    grad_gate = (grad_hid * up_pre * sig * (1.0 + gate_pre * (1.0 - sig))).astype(BF16)
    grad_up = (grad_hid * gate_pre * sig).astype(BF16)
    row = lax.broadcasted_iota(jnp.int32, (count, count), 0)
    col = lax.broadcasted_iota(jnp.int32, (count, count), 1)
    for kind, refs in enumerate((first, second)):
        at = col - kind * (count // 2)
        upper = one_hot((row < count // 2) & (at == row))
        lower = one_hot((row >= count // 2) & (at == row - count // 2))
        hid_rows = dot(upper, hid).astype(BF16)
        gate_rows = dot(lower, grad_gate).astype(BF16)
        up_rows = dot(lower, grad_up).astype(BF16)
        for q in range(QN):
            cols = slice(q * lanes, (q + 1) * lanes)
            term = dot(hid_rows, w_down[:, cols])
            term = term + dot(gate_rows, w_gate[cols, :], ((1,), (1,)))
            term = term + dot(up_rows, w_up[cols, :], ((1,), (1,)))
            each = QN // len(refs)
            refs[q // each][:, q % each * lanes : (q % each + 1) * lanes] = term.astype(BF16)


def pack_kernel(source, here, above, below, out):
    lanes = out.shape[1]
    count = out.shape[0]
    parts = []
    for q in range(QN):
        cols = slice(q * lanes, (q + 1) * lanes)
        summed = here[:, cols].astype(F32) + above[:, cols].astype(F32)
        parts.append(summed + below[:, cols].astype(F32))
    stacked = jnp.concatenate(parts, axis=0).astype(BF16)
    spots = lax.broadcasted_iota(jnp.int32, (count, count), 1)
    out[...] = dot(one_hot(spots == source[...]), stacked).astype(BF16)


def finish_kernel(mine, mixed, grad_tokens, grad_gates):
    lanes = mixed.shape[1] // QN
    topk = grad_gates.shape[1]
    total = mine[0].astype(F32)
    for chip in range(1, mine.shape[0]):
        total = total + mine[chip].astype(F32)
    for q in range(QN):
        cols = slice(q * lanes, (q + 1) * lanes)
        mixed[:, cols] = total[q : q + 1, :lanes].astype(BF16)
        grad_tokens[:, cols] = total[QN + q : QN + q + 1, :lanes].astype(BF16)
    grad_gates[...] = (
        total[0:1, lanes : lanes + topk] + total[0:1, lanes + topk : lanes + 2 * topk]
    )


def local(tokens, expert_ids, gates, w_gate, w_up, w_down, cotangent):
    width = tokens.shape[1]
    lanes = width // QN
    half_width = width // 2
    chips = lax.axis_size(PLANE)
    block = expert_ids.shape[0]
    topk = expert_ids.shape[1]
    core = lax.axis_index("c").astype(jnp.int32)
    expert = lax.axis_index(PLANE).astype(jnp.int32) * 2 + core
    sibling = expert + 1 - 2 * core
    w_gate, w_up, w_down = w_gate[0], w_up[0], w_down[0]

    spread = pl.pallas_call(
        spread_kernel, out_shape=jax.ShapeDtypeStruct((chips, PIECES, lanes), BF16)
    )(tokens, cotangent)
    gathered = lax.all_to_all(spread, PLANE, 0, 0, tiled=True).reshape(chips * PIECES, lanes)

    ids = expert_ids.T
    named = ids == expert
    member = jnp.stack([jnp.any(named, axis=0), jnp.any(ids == sibling, axis=0)])
    token_row = lax.broadcasted_iota(jnp.int32, (block, block), 0)
    token_col = lax.broadcasted_iota(jnp.int32, (block, block), 1)
    earlier = (token_row < token_col).astype(BF16)
    before = dot(member.astype(BF16), earlier)
    place = jnp.where(member, before + 1.0, 0.0)
    spot = lax.broadcasted_iota(jnp.int32, (block, chips * PIECES), 1)
    token_at = lax.broadcasted_iota(jnp.int32, (block, chips * PIECES), 0)
    expand = (token_at == 2 * (spot // PIECES) + core).astype(BF16)
    place_cols = dot(place.astype(BF16), expand)
    row = lax.broadcasted_iota(jnp.int32, (2 * PACK, chips * PIECES), 0)
    col = lax.broadcasted_iota(jnp.int32, (2 * PACK, chips * PIECES), 1)
    held = jnp.where(row < PACK, place_cols[0:1], place_cols[1:2])
    choose = (
        (held == (row % CAP + 1).astype(F32)) & (row // CAP % PIECES == col % PIECES)
    ).astype(BF16)

    gate_of = jnp.sum(jnp.where(named, gates.T.astype(F32), 0.0), axis=0)
    slot_row = lax.broadcasted_iota(jnp.int32, (PACK, block), 0) % CAP + 1
    in_slot = place[0:1] == slot_row.astype(F32)
    gate_rows = jnp.sum(jnp.where(in_slot, gate_of[None], 0.0), axis=1, keepdims=True)
    route_rows = dot(in_slot[:CAP].astype(BF16), named.astype(BF16), ((1,), (1,)))

    chosen = dot(choose, gathered).astype(BF16)
    halves = both_cores(chosen[PACK:])
    packed = chosen[:PACK] + jnp.where(core == 0, halves[1], halves[0])

    zb = lax.axis_index("zb").astype(jnp.int32)
    zd = lax.axis_index("zd").astype(jnp.int32)
    group = ZA * 2 * CAP
    index = jnp.arange(group, dtype=jnp.int32)[:, None]

    def base_of(last):
        at = jnp.where(index < group // 2, 1 - last, last)
        return (index // CAP % ZA * ZB + at) * PACK + index % CAP

    same = lax.all_gather(packed, ("za", "zb"), axis=0, tiled=True)
    middle = same.shape[0] // 2
    from_below = shift_z(same[:middle], 1)
    from_above = shift_z(same[middle:], -1)

    def expert_terms(last, lower, upper, splits):
        width_of = [width // n for n in splits for _ in range(n)]
        return vmem_call(
            expert_kernel,
            [jax.ShapeDtypeStruct((group, w), BF16) for w in width_of],
            cost_estimate=pl.CostEstimate(
                flops=36 * group * width * w_down.shape[0], bytes_accessed=12 * width * w_down.shape[0], transcendentals=0
            ),
        )(base_of(last), lower, upper, w_gate, w_up, w_down)

    far_left, far_right, terms_here = expert_terms(zb, same[:middle], same[middle:], (2, 1))

    back_left = shift_z(far_left, -1)
    back_right = shift_z(far_right, 1)
    terms_below, terms_above = expert_terms(
        jnp.where(zd == 1, 1 - zb, zb), from_below, from_above, (1, 1)
    )
    low = jnp.concatenate(
        [
            (terms_below[:, :half_width].astype(F32) + back_left.astype(F32)).astype(BF16),
            terms_below[:, half_width:],
        ],
        axis=1,
    )
    high = jnp.concatenate(
        [
            terms_above[:, :half_width],
            (terms_above[:, half_width:].astype(F32) + back_right.astype(F32)).astype(BF16),
        ],
        axis=1,
    )
    row = jnp.arange(ZA * PACK, dtype=jnp.int32)[:, None]
    source = (row // CAP % QN) * group + (row // (QN * CAP) % 2 * ZA + row // PACK) * CAP
    outgoing = vmem_call(pack_kernel, jax.ShapeDtypeStruct((ZA * PACK, lanes), BF16))(
        source + row % CAP, terms_here, shift_z(low, -1), shift_z(high, 1)
    ).reshape(ZA, PACK, lanes)
    arrived = lax.all_to_all(outgoing, "za", 0, 0, tiled=True)
    results = jnp.sum(arrived.astype(F32), axis=0)

    half = PACK // 2
    value_rows = results[:half].astype(BF16).astype(F32)
    dots = jnp.sum(value_rows * packed[half:].astype(F32), axis=1)
    slot_dots = jnp.sum(dots.reshape(QN, CAP), axis=0)[:, None]
    dots_high = lax.reduce_precision(slot_dots, 8, 7)
    dots_low = slot_dots - dots_high
    carried = jnp.concatenate([dots_high * route_rows, dots_low * route_rows], axis=1)
    carried = jnp.pad(carried, ((0, PACK - CAP), (0, EXTRA - 2 * topk)))
    scaled = jnp.concatenate([results * gate_rows, carried], axis=1).astype(BF16)
    both = both_cores(scaled).reshape(2 * PACK, lanes + EXTRA)
    swapped = jnp.concatenate([choose[PACK:], choose[:PACK]], axis=0)
    choose_back = jnp.where(core == 0, choose, swapped)

    dense = dot(choose_back, both, ((0,), (0,))).astype(BF16)
    dense = dense.reshape(chips, PIECES, lanes + EXTRA)
    mine = lax.all_to_all(dense, PLANE, 0, 0, tiled=True)
    return pl.pallas_call(
        finish_kernel,
        out_shape=(
            jax.ShapeDtypeStruct((1, width), BF16),
            jax.ShapeDtypeStruct((1, width), BF16),
            jax.ShapeDtypeStruct((1, topk), F32),
        ),
    )(mine)


def solution(mesh, plane=(4, 8, 2)):
    fine = Mesh(mesh.devices.reshape((ZA, ZB, ZD) + plane), ZAXES + PLANE + ("c",))
    rows = P(ZAXES + PLANE + ("c",), None)
    experts = PLANE + ("c",)
    return jax.shard_map(
        local,
        mesh=fine,
        in_specs=(
            rows,
            P(ZAXES, None),
            P(ZAXES, None),
            P(experts, None, ZAXES),
            P(experts, None, ZAXES),
            P(experts, ZAXES, None),
            rows,
        ),
        out_specs=(rows, rows, rows),
        check_vma=False,
    )
```

```python
import jax
import jax.numpy as jnp
import numpy as np
from jax import lax
from jax.experimental import pallas as pl
from jax.experimental.pallas import tpu as pltpu
from jax.sharding import Mesh, PartitionSpec as P

F32 = jnp.float32
BF16 = jnp.bfloat16
CAP = 9
QN = 4
PIECES = 2 * QN
PACK = PIECES * CAP
ZA, ZB, ZD = 4, 2, 2
EXTRA = 128
ZAXES = ("za", "zb", "zd")
PLANE = ("x", "y")


def shift_z(values, step):
    n = ZA * ZB * ZD
    return lax.ppermute(values, ZAXES, [(i, (i + step) % n) for i in range(n)])


def both_cores(values):
    return lax.all_gather(values, "c", axis=0)


def dot(a, b, dims=((1,), (0,))):
    return lax.dot_general(a, b, (dims, ((), ())), preferred_element_type=F32)


def one_hot(mask):
    return mask.astype(F32).astype(BF16)


def spread_kernel(tokens, cotangent, out):
    lanes = out.shape[2]
    rows = [
        ref[:, q * lanes : (q + 1) * lanes] for ref in (tokens, cotangent) for q in range(QN)
    ]
    out[...] = jnp.broadcast_to(jnp.concatenate(rows, axis=0)[None], out.shape)


def expert_kernel(zb_last, low_hbm, high_hbm, gate_hbm, up_hbm, down_hbm, *refs):
    outs, (low, high, w_gate, w_up, w_down, sems) = refs[:-6], refs[-6:]
    loads = [
        pltpu.make_async_copy(source, target, sems.at[i])
        for i, (source, target) in enumerate(
            (
                (low_hbm, low),
                (high_hbm, high),
                (gate_hbm, w_gate),
                (up_hbm, w_up),
                (down_hbm, w_down),
            )
        )
    ]
    for load in loads:
        load.start()
    middle, lanes = low.shape
    hidden = w_down.shape[0]
    kept = middle // PIECES
    padded = (kept + 7) // 8 * 8
    row = lax.broadcasted_iota(jnp.int32, (PIECES * padded, 1), 0)
    at = row % padded
    kind = jnp.where(at < kept // 2, 1 - zb_last[0], zb_last[0])
    place = at % (kept // 2)
    want = ((place // CAP * ZB + kind) * PIECES + row // padded) * CAP + place % CAP
    want = jnp.where(at < kept, want, -1)
    spots = lax.broadcasted_iota(jnp.int32, (PIECES * padded, middle), 1)
    pick = one_hot(spots == want)
    loads[0].wait()
    from_low = dot(pick, low[...])
    loads[1].wait()
    from_high = dot(pick, high[...])

    def rows_of(piece):
        block = slice(piece * padded, (piece + 1) * padded)
        return jnp.concatenate([from_low[block], from_high[block]], axis=0).astype(BF16)

    count = 2 * padded
    pre = jnp.zeros((count, 2 * hidden), F32)
    grad_hid = jnp.zeros((count, hidden), F32)
    for load in loads[2:]:
        load.wait()
    for q in range(QN):
        cols = slice(q * lanes, (q + 1) * lanes)
        pair = jnp.concatenate([w_gate[cols, :], w_up[cols, :]], axis=1)
        pre = pre + dot(rows_of(q), pair)
        grad_hid = grad_hid + dot(rows_of(QN + q), w_down[:, cols], ((1,), (1,)))
    gate_pre, up_pre = pre[:, :hidden], pre[:, hidden:]
    sig = 1.0 / (1.0 + jnp.exp(-gate_pre))
    hid = (gate_pre * sig * up_pre).astype(BF16)
    grad_gate = (grad_hid * up_pre * sig * (1.0 + gate_pre * (1.0 - sig))).astype(BF16)
    grad_up = (grad_hid * gate_pre * sig).astype(BF16)
    grads = jnp.concatenate([grad_gate, grad_up], axis=1)
    group = 2 * ZA * CAP
    back = lax.broadcasted_iota(jnp.int32, (2 * group, 1), 0)
    za = back // CAP % ZA
    source = za // 2 * padded + back // group * (kept // 2) + za % 2 * CAP + back % CAP
    second = back // (ZA * CAP) % 2
    taken = lax.broadcasted_iota(jnp.int32, (2 * group, count), 1)
    hid_rows = dot(one_hot(taken == jnp.where(second == 0, source, -1)), hid).astype(BF16)
    grad_rows = dot(one_hot(taken == jnp.where(second == 1, source, -1)), grads).astype(BF16)
    first, last = outs[: len(outs) // 2 + len(outs) % 2], outs[-(len(outs) // 2) :]
    for q in range(QN):
        cols = slice(q * lanes, (q + 1) * lanes)
        pair = jnp.concatenate([w_gate[cols, :], w_up[cols, :]], axis=1)
        term = dot(hid_rows, w_down[:, cols]) + dot(grad_rows, pair, ((1,), (1,)))
        for kind, parts in enumerate((first, last)):
            each = QN // len(parts)
            target = slice(q % each * lanes, (q % each + 1) * lanes)
            parts[q // each][:, target] = term[kind * group : (kind + 1) * group].astype(BF16)


def pack_kernel(source, here, above, below, out):
    lanes = out.shape[1]
    count = out.shape[0]
    parts = []
    for q in range(QN):
        cols = slice(q * lanes, (q + 1) * lanes)
        summed = here[:, cols].astype(F32) + above[:, cols].astype(F32)
        parts.append(summed + below[:, cols].astype(F32))
    stacked = jnp.concatenate(parts, axis=0).astype(BF16)
    spots = lax.broadcasted_iota(jnp.int32, (count, count), 1)
    out[...] = dot(one_hot(spots == source[...]), stacked).astype(BF16)


def finish_kernel(mine, mixed, grad_tokens, grad_gates):
    lanes = mixed.shape[1] // QN
    topk = grad_gates.shape[1]
    total = mine[0].astype(F32)
    for chip in range(1, mine.shape[0]):
        total = total + mine[chip].astype(F32)
    for q in range(QN):
        cols = slice(q * lanes, (q + 1) * lanes)
        mixed[:, cols] = total[q : q + 1, :lanes].astype(BF16)
        grad_tokens[:, cols] = total[QN + q : QN + q + 1, :lanes].astype(BF16)
    grad_gates[...] = (
        total[0:1, lanes : lanes + topk] + total[0:1, lanes + topk : lanes + 2 * topk]
    )


def local(tokens, expert_ids, gates, w_gate, w_up, w_down, cotangent):
    width = tokens.shape[1]
    lanes = width // QN
    half_width = width // 2
    chips = lax.axis_size(PLANE)
    block = expert_ids.shape[0]
    topk = expert_ids.shape[1]
    core = lax.axis_index("c").astype(jnp.int32)
    expert = lax.axis_index(PLANE).astype(jnp.int32) * 2 + core
    sibling = expert + 1 - 2 * core
    w_gate, w_up, w_down = w_gate[0], w_up[0], w_down[0]

    spread = pl.pallas_call(
        spread_kernel, out_shape=jax.ShapeDtypeStruct((chips, PIECES, lanes), BF16)
    )(tokens, cotangent)
    gathered = lax.all_to_all(spread, PLANE, 0, 0, tiled=True).reshape(chips * PIECES, lanes)

    ids = expert_ids.T
    named = ids == expert
    member = jnp.stack([jnp.any(named, axis=0), jnp.any(ids == sibling, axis=0)])
    token_row = lax.broadcasted_iota(jnp.int32, (block, block), 0)
    token_col = lax.broadcasted_iota(jnp.int32, (block, block), 1)
    earlier = (token_row < token_col).astype(BF16)
    before = dot(member.astype(BF16), earlier)
    place = jnp.where(member, before + 1.0, 0.0)
    spot = lax.broadcasted_iota(jnp.int32, (block, chips * PIECES), 1)
    token_at = lax.broadcasted_iota(jnp.int32, (block, chips * PIECES), 0)
    expand = (token_at == 2 * (spot // PIECES) + core).astype(BF16)
    place_cols = dot(place.astype(BF16), expand)
    row = lax.broadcasted_iota(jnp.int32, (2 * PACK, chips * PIECES), 0)
    col = lax.broadcasted_iota(jnp.int32, (2 * PACK, chips * PIECES), 1)
    held = jnp.where(row < PACK, place_cols[0:1], place_cols[1:2])
    choose = (
        (held == (row % CAP + 1).astype(F32)) & (row // CAP % PIECES == col % PIECES)
    ).astype(BF16)

    gate_of = jnp.sum(jnp.where(named, gates.T.astype(F32), 0.0), axis=0)
    slot_row = lax.broadcasted_iota(jnp.int32, (PACK, block), 0) % CAP + 1
    in_slot = place[0:1] == slot_row.astype(F32)
    gate_rows = jnp.sum(jnp.where(in_slot, gate_of[None], 0.0), axis=1, keepdims=True)
    route_rows = dot(in_slot[:CAP].astype(BF16), named.astype(BF16), ((1,), (1,)))

    chosen = dot(choose, gathered).astype(BF16)
    halves = both_cores(chosen[PACK:])
    packed = chosen[:PACK] + jnp.where(core == 0, halves[1], halves[0])

    zb = lax.axis_index("zb").astype(jnp.int32)
    zd = lax.axis_index("zd").astype(jnp.int32)
    group = ZA * 2 * CAP
    same = lax.all_gather(packed, ("za", "zb"), axis=0, tiled=True)
    middle = same.shape[0] // 2
    from_below = shift_z(same[:middle], 1)
    from_above = shift_z(same[middle:], -1)

    def expert_terms(last, lower, upper, splits):
        width_of = [width // n for n in splits for _ in range(n)]
        weights = (w_gate, w_up, w_down)
        hbm = pl.BlockSpec(memory_space=pl.ANY)
        return pl.pallas_call(
            expert_kernel,
            out_shape=[jax.ShapeDtypeStruct((group, w), BF16) for w in width_of],
            in_specs=[pl.BlockSpec(memory_space=pltpu.SMEM)] + [hbm] * 5,
            scratch_shapes=[pltpu.VMEM(v.shape, BF16) for v in (lower, upper) + weights]
            + [pltpu.SemaphoreType.DMA((5,))],
            compiler_params=pltpu.CompilerParams(vmem_limit_bytes=62 * 2**20),
            cost_estimate=pl.CostEstimate(
                flops=36 * group * width * w_down.shape[0],
                bytes_accessed=12 * width * w_down.shape[0],
                transcendentals=0,
            ),
        )(last[None], lower, upper, *weights)

    far_left, far_right, terms_here = expert_terms(zb, same[:middle], same[middle:], (2, 1))

    back_left = shift_z(far_left, -1)
    back_right = shift_z(far_right, 1)
    terms_below, terms_above = expert_terms(
        jnp.where(zd == 1, 1 - zb, zb), from_below, from_above, (1, 1)
    )
    low = jnp.concatenate(
        [
            (terms_below[:, :half_width].astype(F32) + back_left.astype(F32)).astype(BF16),
            terms_below[:, half_width:],
        ],
        axis=1,
    )
    high = jnp.concatenate(
        [
            terms_above[:, :half_width],
            (terms_above[:, half_width:].astype(F32) + back_right.astype(F32)).astype(BF16),
        ],
        axis=1,
    )
    row = jnp.arange(ZA * PACK, dtype=jnp.int32)[:, None]
    source = (row // CAP % QN) * group + (row // (QN * CAP) % 2 * ZA + row // PACK) * CAP
    outgoing = pl.pallas_call(
        pack_kernel,
        out_shape=jax.ShapeDtypeStruct((ZA * PACK, lanes), BF16),
        compiler_params=pltpu.CompilerParams(vmem_limit_bytes=16 * 2**20),
    )(
        source + row % CAP, terms_here, shift_z(low, -1), shift_z(high, 1)
    ).reshape(ZA, PACK, lanes)
    arrived = lax.all_to_all(outgoing, "za", 0, 0, tiled=True)
    results = jnp.sum(arrived.astype(F32), axis=0)

    half = PACK // 2
    value_rows = results[:half].astype(BF16).astype(F32)
    dots = jnp.sum(value_rows * packed[half:].astype(F32), axis=1)
    slot_dots = jnp.sum(dots.reshape(QN, CAP), axis=0)[:, None]
    dots_high = lax.reduce_precision(slot_dots, 8, 7)
    dots_low = slot_dots - dots_high
    carried = jnp.concatenate([dots_high * route_rows, dots_low * route_rows], axis=1)
    carried = jnp.pad(carried, ((0, PACK - CAP), (0, EXTRA - 2 * topk)))
    scaled = jnp.concatenate([results * gate_rows, carried], axis=1).astype(BF16)
    both = both_cores(scaled).reshape(2 * PACK, lanes + EXTRA)
    swapped = jnp.concatenate([choose[PACK:], choose[:PACK]], axis=0)
    choose_back = jnp.where(core == 0, choose, swapped)

    dense = dot(choose_back, both, ((0,), (0,))).astype(BF16)
    dense = dense.reshape(chips, PIECES, lanes + EXTRA)
    mine = lax.all_to_all(dense, PLANE, 0, 0, tiled=True)
    return pl.pallas_call(
        finish_kernel,
        out_shape=(
            jax.ShapeDtypeStruct((1, width), BF16),
            jax.ShapeDtypeStruct((1, width), BF16),
            jax.ShapeDtypeStruct((1, topk), F32),
        ),
    )(mine)


def solution(mesh, plane=(4, 8, 2)):
    fine = Mesh(mesh.devices.reshape((ZA, ZB, ZD) + plane), ZAXES + PLANE + ("c",))
    rows = P(ZAXES + PLANE + ("c",), None)
    experts = PLANE + ("c",)
    return jax.shard_map(
        local,
        mesh=fine,
        in_specs=(
            rows,
            P(ZAXES, None),
            P(ZAXES, None),
            P(experts, None, ZAXES),
            P(experts, None, ZAXES),
            P(experts, ZAXES, None),
            rows,
        ),
        out_specs=(rows, rows, rows),
        check_vma=False,
    )
```

```python
import jax
import jax.numpy as jnp
import numpy as np
from jax import lax
from jax.experimental import pallas as pl
from jax.experimental.pallas import tpu as pltpu
from jax.sharding import Mesh, PartitionSpec as P

F32 = jnp.float32
BF16 = jnp.bfloat16
CAP = 9
QN = 4
PIECES = 2 * QN
PACK = PIECES * CAP
ZA, ZB, ZD = 4, 2, 2
EXTRA = 128
ZAXES = ("za", "zb", "zd")
PLANE = ("x", "y")


def shift_z(values, step):
    n = ZA * ZB * ZD
    return lax.ppermute(values, ZAXES, [(i, (i + step) % n) for i in range(n)])


def both_cores(values):
    return lax.all_gather(values, "c", axis=0)


def dot(a, b, dims=((1,), (0,))):
    return lax.dot_general(a, b, (dims, ((), ())), preferred_element_type=F32)


def one_hot(mask):
    return mask.astype(F32).astype(BF16)


def spread_kernel(tokens, cotangent, out):
    lanes = out.shape[2]
    rows = [
        ref[:, q * lanes : (q + 1) * lanes] for ref in (tokens, cotangent) for q in range(QN)
    ]
    out[...] = jnp.broadcast_to(jnp.concatenate(rows, axis=0)[None], out.shape)


def expert_kernel(zb_last, low, high, w_gate, w_up, w_down, *outs):
    middle, lanes = low.shape
    hidden = w_down.shape[0]
    kept = middle // PIECES
    padded = (kept + 7) // 8 * 8
    row = lax.broadcasted_iota(jnp.int32, (PIECES * padded, 1), 0)
    at = row % padded
    kind = jnp.where(at < kept // 2, 1 - zb_last[0], zb_last[0])
    place = at % (kept // 2)
    want = ((place // CAP * ZB + kind) * PIECES + row // padded) * CAP + place % CAP
    want = jnp.where(at < kept, want, -1)
    spots = lax.broadcasted_iota(jnp.int32, (PIECES * padded, middle), 1)
    pick = one_hot(spots == want)
    from_low = dot(pick, low[...])
    from_high = dot(pick, high[...])

    def rows_of(piece):
        block = slice(piece * padded, (piece + 1) * padded)
        return jnp.concatenate([from_low[block], from_high[block]], axis=0).astype(BF16)

    count = 2 * padded
    pre = jnp.zeros((count, 2 * hidden), F32)
    grad_hid = jnp.zeros((count, hidden), F32)
    for q in range(QN):
        cols = slice(q * lanes, (q + 1) * lanes)
        pair = jnp.concatenate([w_gate[cols, :], w_up[cols, :]], axis=1)
        pre = pre + dot(rows_of(q), pair)
        grad_hid = grad_hid + dot(rows_of(QN + q), w_down[:, cols], ((1,), (1,)))
    gate_pre, up_pre = pre[:, :hidden], pre[:, hidden:]
    sig = 1.0 / (1.0 + jnp.exp(-gate_pre))
    hid = (gate_pre * sig * up_pre).astype(BF16)
    grad_gate = (grad_hid * up_pre * sig * (1.0 + gate_pre * (1.0 - sig))).astype(BF16)
    grad_up = (grad_hid * gate_pre * sig).astype(BF16)
    grads = jnp.concatenate([grad_gate, grad_up], axis=1)
    group = 2 * ZA * CAP
    back = lax.broadcasted_iota(jnp.int32, (2 * group, 1), 0)
    za = back // CAP % ZA
    source = za // 2 * padded + back // group * (kept // 2) + za % 2 * CAP + back % CAP
    second = back // (ZA * CAP) % 2
    taken = lax.broadcasted_iota(jnp.int32, (2 * group, count), 1)
    hid_rows = dot(one_hot(taken == jnp.where(second == 0, source, -1)), hid).astype(BF16)
    grad_rows = dot(one_hot(taken == jnp.where(second == 1, source, -1)), grads).astype(BF16)
    first, last = outs[: len(outs) // 2 + len(outs) % 2], outs[-(len(outs) // 2) :]
    for q in range(QN):
        cols = slice(q * lanes, (q + 1) * lanes)
        pair = jnp.concatenate([w_gate[cols, :], w_up[cols, :]], axis=1)
        term = dot(hid_rows, w_down[:, cols]) + dot(grad_rows, pair, ((1,), (1,)))
        for kind, parts in enumerate((first, last)):
            each = QN // len(parts)
            target = slice(q % each * lanes, (q % each + 1) * lanes)
            parts[q // each][:, target] = term[kind * group : (kind + 1) * group].astype(BF16)


def pack_kernel(source, here, above, below, out):
    lanes = out.shape[1]
    count = out.shape[0]
    parts = []
    for q in range(QN):
        cols = slice(q * lanes, (q + 1) * lanes)
        summed = here[:, cols].astype(F32) + above[:, cols].astype(F32)
        parts.append(summed + below[:, cols].astype(F32))
    stacked = jnp.concatenate(parts, axis=0).astype(BF16)
    spots = lax.broadcasted_iota(jnp.int32, (count, count), 1)
    out[...] = dot(one_hot(spots == source[...]), stacked).astype(BF16)


def finish_kernel(mine, mixed, grad_tokens, grad_gates):
    lanes = mixed.shape[1] // QN
    topk = grad_gates.shape[1]
    total = mine[0].astype(F32)
    for chip in range(1, mine.shape[0]):
        total = total + mine[chip].astype(F32)
    for q in range(QN):
        cols = slice(q * lanes, (q + 1) * lanes)
        mixed[:, cols] = total[q : q + 1, :lanes].astype(BF16)
        grad_tokens[:, cols] = total[QN + q : QN + q + 1, :lanes].astype(BF16)
    grad_gates[...] = (
        total[0:1, lanes : lanes + topk] + total[0:1, lanes + topk : lanes + 2 * topk]
    )


def local(tokens, expert_ids, gates, w_gate, w_up, w_down, cotangent):
    width = tokens.shape[1]
    lanes = width // QN
    half_width = width // 2
    chips = lax.axis_size(PLANE)
    block = expert_ids.shape[0]
    topk = expert_ids.shape[1]
    core = lax.axis_index("c").astype(jnp.int32)
    expert = lax.axis_index(PLANE).astype(jnp.int32) * 2 + core
    sibling = expert + 1 - 2 * core
    w_gate, w_up, w_down = w_gate[0], w_up[0], w_down[0]

    spread = pl.pallas_call(
        spread_kernel, out_shape=jax.ShapeDtypeStruct((chips, PIECES, lanes), BF16)
    )(tokens, cotangent)
    gathered = lax.all_to_all(spread, PLANE, 0, 0, tiled=True).reshape(chips * PIECES, lanes)

    ids = expert_ids.T
    named = ids == expert
    member = jnp.stack([jnp.any(named, axis=0), jnp.any(ids == sibling, axis=0)])
    token_row = lax.broadcasted_iota(jnp.int32, (block, block), 0)
    token_col = lax.broadcasted_iota(jnp.int32, (block, block), 1)
    earlier = (token_row < token_col).astype(BF16)
    before = dot(member.astype(BF16), earlier)
    place = jnp.where(member, before + 1.0, 0.0)
    spot = lax.broadcasted_iota(jnp.int32, (block, chips * PIECES), 1)
    token_at = lax.broadcasted_iota(jnp.int32, (block, chips * PIECES), 0)
    expand = (token_at == 2 * (spot // PIECES) + core).astype(BF16)
    place_cols = dot(place.astype(BF16), expand)
    row = lax.broadcasted_iota(jnp.int32, (2 * PACK, chips * PIECES), 0)
    col = lax.broadcasted_iota(jnp.int32, (2 * PACK, chips * PIECES), 1)
    held = jnp.where(row < PACK, place_cols[0:1], place_cols[1:2])
    choose = (
        (held == (row % CAP + 1).astype(F32)) & (row // CAP % PIECES == col % PIECES)
    ).astype(BF16)

    gate_of = jnp.sum(jnp.where(named, gates.T.astype(F32), 0.0), axis=0)
    slot_row = lax.broadcasted_iota(jnp.int32, (PACK, block), 0) % CAP + 1
    in_slot = place[0:1] == slot_row.astype(F32)
    gate_rows = jnp.sum(jnp.where(in_slot, gate_of[None], 0.0), axis=1, keepdims=True)
    route_rows = dot(in_slot[:CAP].astype(BF16), named.astype(BF16), ((1,), (1,)))

    chosen = dot(choose, gathered).astype(BF16)
    halves = both_cores(chosen[PACK:])
    packed = chosen[:PACK] + jnp.where(core == 0, halves[1], halves[0])

    zb = lax.axis_index("zb").astype(jnp.int32)
    zd = lax.axis_index("zd").astype(jnp.int32)
    group = ZA * 2 * CAP
    same = lax.all_gather(packed, ("za", "zb"), axis=0, tiled=True)
    middle = same.shape[0] // 2
    from_below = shift_z(same[:middle], 1)
    from_above = shift_z(same[middle:], -1)

    def expert_terms(last, lower, upper, splits):
        width_of = [width // n for n in splits for _ in range(n)]
        weights = (w_gate, w_up, w_down)
        return pl.pallas_call(
            expert_kernel,
            out_shape=[jax.ShapeDtypeStruct((group, w), BF16) for w in width_of],
            in_specs=[pl.BlockSpec(memory_space=pltpu.SMEM)] + [pl.BlockSpec()] * 5,
            compiler_params=pltpu.CompilerParams(vmem_limit_bytes=16 * 2**20),
            cost_estimate=pl.CostEstimate(
                flops=36 * group * width * w_down.shape[0],
                bytes_accessed=12 * width * w_down.shape[0],
                transcendentals=0,
            ),
        )(last[None], lower, upper, *weights)

    far_left, far_right, terms_here = expert_terms(zb, same[:middle], same[middle:], (2, 1))

    back_left = shift_z(far_left, -1)
    back_right = shift_z(far_right, 1)
    terms_below, terms_above = expert_terms(
        jnp.where(zd == 1, 1 - zb, zb), from_below, from_above, (1, 1)
    )
    low = lax.dynamic_update_slice(
        terms_below,
        (terms_below[:, :half_width].astype(F32) + back_left.astype(F32)).astype(BF16),
        (0, 0),
    )
    high = lax.dynamic_update_slice(
        terms_above,
        (terms_above[:, half_width:].astype(F32) + back_right.astype(F32)).astype(BF16),
        (0, half_width),
    )
    row = jnp.arange(ZA * PACK, dtype=jnp.int32)[:, None]
    source = (row // CAP % QN) * group + (row // (QN * CAP) % 2 * ZA + row // PACK) * CAP
    outgoing = pl.pallas_call(
        pack_kernel,
        out_shape=jax.ShapeDtypeStruct((ZA * PACK, lanes), BF16),
        compiler_params=pltpu.CompilerParams(vmem_limit_bytes=16 * 2**20),
    )(
        source + row % CAP, terms_here, shift_z(low, -1), shift_z(high, 1)
    ).reshape(ZA, PACK, lanes)
    arrived = lax.all_to_all(outgoing, "za", 0, 0, tiled=True)
    results = jnp.sum(arrived.astype(F32), axis=0)

    half = PACK // 2
    value_rows = results[:half].astype(BF16).astype(F32)
    dots = jnp.sum(value_rows * packed[half:].astype(F32), axis=1)
    slot_dots = jnp.sum(dots.reshape(QN, CAP), axis=0)[:, None]
    dots_high = lax.reduce_precision(slot_dots, 8, 7)
    dots_low = slot_dots - dots_high
    carried = jnp.concatenate([dots_high * route_rows, dots_low * route_rows], axis=1)
    carried = jnp.pad(carried, ((0, PACK - CAP), (0, EXTRA - 2 * topk)))
    scaled = jnp.concatenate([results * gate_rows, carried], axis=1).astype(BF16)
    both = both_cores(scaled).reshape(2 * PACK, lanes + EXTRA)
    swapped = jnp.concatenate([choose[PACK:], choose[:PACK]], axis=0)
    choose_back = jnp.where(core == 0, choose, swapped)

    dense = dot(choose_back, both, ((0,), (0,))).astype(BF16)
    dense = dense.reshape(chips, PIECES, lanes + EXTRA)
    mine = lax.all_to_all(dense, PLANE, 0, 0, tiled=True)
    return pl.pallas_call(
        finish_kernel,
        out_shape=(
            jax.ShapeDtypeStruct((1, width), BF16),
            jax.ShapeDtypeStruct((1, width), BF16),
            jax.ShapeDtypeStruct((1, topk), F32),
        ),
    )(mine)


def solution(mesh, plane=(4, 8, 2)):
    fine = Mesh(mesh.devices.reshape((ZA, ZB, ZD) + plane), ZAXES + PLANE + ("c",))
    rows = P(ZAXES + PLANE + ("c",), None)
    experts = PLANE + ("c",)
    return jax.shard_map(
        local,
        mesh=fine,
        in_specs=(
            rows,
            P(ZAXES, None),
            P(ZAXES, None),
            P(experts, None, ZAXES),
            P(experts, None, ZAXES),
            P(experts, ZAXES, None),
            rows,
        ),
        out_specs=(rows, rows, rows),
        check_vma=False,
    )
```

```python
import jax
import jax.numpy as jnp
import numpy as np
from jax import lax
from jax.experimental import pallas as pl
from jax.experimental.pallas import tpu as pltpu
from jax.sharding import Mesh, PartitionSpec as P

F32 = jnp.float32
BF16 = jnp.bfloat16
CAP = 9
QN = 4
PIECES = 2 * QN
PACK = PIECES * CAP
ZA, ZB, ZD = 4, 2, 2
EXTRA = 128
ZAXES = ("za", "zb", "zd")
PLANE = ("x", "y")


def shift_z(values, step):
    n = ZA * ZB * ZD
    return lax.ppermute(values, ZAXES, [(i, (i + step) % n) for i in range(n)])


def both_cores(values):
    return lax.all_gather(values, "c", axis=0)


def dot(a, b, dims=((1,), (0,))):
    return lax.dot_general(a, b, (dims, ((), ())), preferred_element_type=F32)


def one_hot(mask):
    return mask.astype(F32).astype(BF16)


def spread_kernel(tokens, cotangent, out):
    lanes = out.shape[2]
    rows = [
        ref[:, q * lanes : (q + 1) * lanes] for ref in (tokens, cotangent) for q in range(QN)
    ]
    out[...] = jnp.broadcast_to(jnp.concatenate(rows, axis=0)[None], out.shape)


def expert_kernel(zb_last, low_hbm, high_hbm, gate_hbm, up_hbm, down_hbm, *refs):
    outs, (low, high, w_gate, w_up, w_down, stage, sems, out_sems) = refs[:-8], refs[-8:]
    loads = [
        pltpu.make_async_copy(source, target, sems.at[i])
        for i, (source, target) in enumerate(
            (
                (low_hbm, low),
                (high_hbm, high),
                (gate_hbm, w_gate),
                (up_hbm, w_up),
                (down_hbm, w_down),
            )
        )
    ]
    for load in loads:
        load.start()
    middle, lanes = low.shape
    hidden = w_down.shape[0]
    kept = middle // PIECES
    padded = (kept + 7) // 8 * 8
    row = lax.broadcasted_iota(jnp.int32, (PIECES * padded, 1), 0)
    at = row % padded
    kind = jnp.where(at < kept // 2, 1 - zb_last[0], zb_last[0])
    place = at % (kept // 2)
    want = ((place // CAP * ZB + kind) * PIECES + row // padded) * CAP + place % CAP
    want = jnp.where(at < kept, want, -1)
    spots = lax.broadcasted_iota(jnp.int32, (PIECES * padded, middle), 1)
    pick = one_hot(spots == want)
    loads[0].wait()
    from_low = dot(pick, low[...])
    loads[1].wait()
    from_high = dot(pick, high[...])

    def rows_of(piece):
        block = slice(piece * padded, (piece + 1) * padded)
        return jnp.concatenate([from_low[block], from_high[block]], axis=0).astype(BF16)

    count = 2 * padded
    pre = jnp.zeros((count, 2 * hidden), F32)
    grad_hid = jnp.zeros((count, hidden), F32)
    for load in loads[2:]:
        load.wait()
    for q in range(QN):
        cols = slice(q * lanes, (q + 1) * lanes)
        pair = jnp.concatenate([w_gate[cols, :], w_up[cols, :]], axis=1)
        pre = pre + dot(rows_of(q), pair)
        grad_hid = grad_hid + dot(rows_of(QN + q), w_down[:, cols], ((1,), (1,)))
    gate_pre, up_pre = pre[:, :hidden], pre[:, hidden:]
    sig = 1.0 / (1.0 + jnp.exp(-gate_pre))
    hid = (gate_pre * sig * up_pre).astype(BF16)
    grad_gate = (grad_hid * up_pre * sig * (1.0 + gate_pre * (1.0 - sig))).astype(BF16)
    grad_up = (grad_hid * gate_pre * sig).astype(BF16)
    grads = jnp.concatenate([grad_gate, grad_up], axis=1)
    group = 2 * ZA * CAP
    back = lax.broadcasted_iota(jnp.int32, (2 * group, 1), 0)
    za = back // CAP % ZA
    source = za // 2 * padded + back // group * (kept // 2) + za % 2 * CAP + back % CAP
    second = back // (ZA * CAP) % 2
    taken = lax.broadcasted_iota(jnp.int32, (2 * group, count), 1)
    hid_rows = dot(one_hot(taken == jnp.where(second == 0, source, -1)), hid).astype(BF16)
    grad_rows = dot(one_hot(taken == jnp.where(second == 1, source, -1)), grads).astype(BF16)
    first, last = outs[: len(outs) // 2 + len(outs) % 2], outs[-(len(outs) // 2) :]
    stores = []
    for q in range(QN):
        cols = slice(q * lanes, (q + 1) * lanes)
        pair = jnp.concatenate([w_gate[cols, :], w_up[cols, :]], axis=1)
        term = dot(hid_rows, w_down[:, cols]) + dot(grad_rows, pair, ((1,), (1,)))
        for kind, parts in enumerate((first, last)):
            each = QN // len(parts)
            target = slice(q % each * lanes, (q % each + 1) * lanes)
            stage[kind, q] = term[kind * group : (kind + 1) * group].astype(BF16)
            store = pltpu.make_async_copy(
                stage.at[kind, q], parts[q // each].at[:, target], out_sems.at[kind, q]
            )
            store.start()
            stores.append(store)
    for store in stores:
        store.wait()


def pack_kernel(source, here, above, below, out):
    lanes = out.shape[1]
    count = out.shape[0]
    parts = []
    for q in range(QN):
        cols = slice(q * lanes, (q + 1) * lanes)
        summed = here[:, cols].astype(F32) + above[:, cols].astype(F32)
        parts.append(summed + below[:, cols].astype(F32))
    stacked = jnp.concatenate(parts, axis=0).astype(BF16)
    spots = lax.broadcasted_iota(jnp.int32, (count, count), 1)
    out[...] = dot(one_hot(spots == source[...]), stacked).astype(BF16)


def finish_kernel(mine, mixed, grad_tokens, grad_gates):
    lanes = mixed.shape[1] // QN
    topk = grad_gates.shape[1]
    total = mine[0].astype(F32)
    for chip in range(1, mine.shape[0]):
        total = total + mine[chip].astype(F32)
    for q in range(QN):
        cols = slice(q * lanes, (q + 1) * lanes)
        mixed[:, cols] = total[q : q + 1, :lanes].astype(BF16)
        grad_tokens[:, cols] = total[QN + q : QN + q + 1, :lanes].astype(BF16)
    grad_gates[...] = (
        total[0:1, lanes : lanes + topk] + total[0:1, lanes + topk : lanes + 2 * topk]
    )


def local(tokens, expert_ids, gates, w_gate, w_up, w_down, cotangent):
    width = tokens.shape[1]
    lanes = width // QN
    half_width = width // 2
    chips = lax.axis_size(PLANE)
    block = expert_ids.shape[0]
    topk = expert_ids.shape[1]
    core = lax.axis_index("c").astype(jnp.int32)
    expert = lax.axis_index(PLANE).astype(jnp.int32) * 2 + core
    sibling = expert + 1 - 2 * core
    w_gate, w_up, w_down = w_gate[0], w_up[0], w_down[0]

    spread = pl.pallas_call(
        spread_kernel, out_shape=jax.ShapeDtypeStruct((chips, PIECES, lanes), BF16)
    )(tokens, cotangent)
    gathered = lax.all_to_all(spread, PLANE, 0, 0, tiled=True).reshape(chips * PIECES, lanes)

    ids = expert_ids.T
    named = ids == expert
    member = jnp.stack([jnp.any(named, axis=0), jnp.any(ids == sibling, axis=0)])
    token_row = lax.broadcasted_iota(jnp.int32, (block, block), 0)
    token_col = lax.broadcasted_iota(jnp.int32, (block, block), 1)
    earlier = (token_row < token_col).astype(BF16)
    before = dot(member.astype(BF16), earlier)
    place = jnp.where(member, before + 1.0, 0.0)
    spot = lax.broadcasted_iota(jnp.int32, (block, chips * PIECES), 1)
    token_at = lax.broadcasted_iota(jnp.int32, (block, chips * PIECES), 0)
    expand = (token_at == 2 * (spot // PIECES) + core).astype(BF16)
    place_cols = dot(place.astype(BF16), expand)
    row = lax.broadcasted_iota(jnp.int32, (2 * PACK, chips * PIECES), 0)
    col = lax.broadcasted_iota(jnp.int32, (2 * PACK, chips * PIECES), 1)
    held = jnp.where(row < PACK, place_cols[0:1], place_cols[1:2])
    choose = (
        (held == (row % CAP + 1).astype(F32)) & (row // CAP % PIECES == col % PIECES)
    ).astype(BF16)

    gate_of = jnp.sum(jnp.where(named, gates.T.astype(F32), 0.0), axis=0)
    slot_row = lax.broadcasted_iota(jnp.int32, (PACK, block), 0) % CAP + 1
    in_slot = place[0:1] == slot_row.astype(F32)
    gate_rows = jnp.sum(jnp.where(in_slot, gate_of[None], 0.0), axis=1, keepdims=True)
    route_rows = dot(in_slot[:CAP].astype(BF16), named.astype(BF16), ((1,), (1,)))

    chosen = dot(choose, gathered).astype(BF16)
    halves = both_cores(chosen[PACK:])
    packed = chosen[:PACK] + jnp.where(core == 0, halves[1], halves[0])

    zb = lax.axis_index("zb").astype(jnp.int32)
    zd = lax.axis_index("zd").astype(jnp.int32)
    group = ZA * 2 * CAP
    same = lax.all_gather(packed, ("za", "zb"), axis=0, tiled=True)
    middle = same.shape[0] // 2
    from_below = shift_z(same[:middle], 1)
    from_above = shift_z(same[middle:], -1)

    def expert_terms(last, lower, upper, splits):
        width_of = [width // n for n in splits for _ in range(n)]
        weights = (w_gate, w_up, w_down)
        hbm = pl.BlockSpec(memory_space=pl.ANY)
        return pl.pallas_call(
            expert_kernel,
            out_shape=[jax.ShapeDtypeStruct((group, w), BF16) for w in width_of],
            in_specs=[pl.BlockSpec(memory_space=pltpu.SMEM)] + [hbm] * 5,
            scratch_shapes=[pltpu.VMEM(v.shape, BF16) for v in (lower, upper) + weights]
            + [pltpu.VMEM((2, QN, group, lanes), BF16)]
            + [pltpu.SemaphoreType.DMA((5,)), pltpu.SemaphoreType.DMA((2, QN))],
            out_specs=[hbm for _ in width_of],
            compiler_params=pltpu.CompilerParams(vmem_limit_bytes=62 * 2**20),
            cost_estimate=pl.CostEstimate(
                flops=36 * group * width * w_down.shape[0],
                bytes_accessed=12 * width * w_down.shape[0],
                transcendentals=0,
            ),
        )(last[None], lower, upper, *weights)

    far_left, far_right, terms_here = expert_terms(zb, same[:middle], same[middle:], (2, 1))

    back_left = shift_z(far_left, -1)
    back_right = shift_z(far_right, 1)
    below_left, below_right, above_left, above_right = expert_terms(
        jnp.where(zd == 1, 1 - zb, zb), from_below, from_above, (2, 2)
    )
    met_left = (below_left.astype(F32) + back_left.astype(F32)).astype(BF16)
    met_right = (above_right.astype(F32) + back_right.astype(F32)).astype(BF16)
    low = jnp.concatenate([met_left, below_right], axis=1)
    high = jnp.concatenate([above_left, met_right], axis=1)
    row = jnp.arange(ZA * PACK, dtype=jnp.int32)[:, None]
    source = (row // CAP % QN) * group + (row // (QN * CAP) % 2 * ZA + row // PACK) * CAP
    outgoing = pl.pallas_call(
        pack_kernel,
        out_shape=jax.ShapeDtypeStruct((ZA * PACK, lanes), BF16),
        compiler_params=pltpu.CompilerParams(vmem_limit_bytes=16 * 2**20),
    )(
        source + row % CAP, terms_here, shift_z(low, -1), shift_z(high, 1)
    ).reshape(ZA, PACK, lanes)
    arrived = lax.all_to_all(outgoing, "za", 0, 0, tiled=True)
    results = jnp.sum(arrived.astype(F32), axis=0)

    half = PACK // 2
    value_rows = results[:half].astype(BF16).astype(F32)
    dots = jnp.sum(value_rows * packed[half:].astype(F32), axis=1)
    slot_dots = jnp.sum(dots.reshape(QN, CAP), axis=0)[:, None]
    dots_high = lax.reduce_precision(slot_dots, 8, 7)
    dots_low = slot_dots - dots_high
    carried = jnp.concatenate([dots_high * route_rows, dots_low * route_rows], axis=1)
    carried = jnp.pad(carried, ((0, PACK - CAP), (0, EXTRA - 2 * topk)))
    scaled = jnp.concatenate([results * gate_rows, carried], axis=1).astype(BF16)
    both = both_cores(scaled).reshape(2 * PACK, lanes + EXTRA)
    swapped = jnp.concatenate([choose[PACK:], choose[:PACK]], axis=0)
    choose_back = jnp.where(core == 0, choose, swapped)

    dense = dot(choose_back, both, ((0,), (0,))).astype(BF16)
    dense = dense.reshape(chips, PIECES, lanes + EXTRA)
    mine = lax.all_to_all(dense, PLANE, 0, 0, tiled=True)
    return pl.pallas_call(
        finish_kernel,
        out_shape=(
            jax.ShapeDtypeStruct((1, width), BF16),
            jax.ShapeDtypeStruct((1, width), BF16),
            jax.ShapeDtypeStruct((1, topk), F32),
        ),
    )(mine)


def solution(mesh, plane=(4, 8, 2)):
    fine = Mesh(mesh.devices.reshape((ZA, ZB, ZD) + plane), ZAXES + PLANE + ("c",))
    rows = P(ZAXES + PLANE + ("c",), None)
    experts = PLANE + ("c",)
    return jax.shard_map(
        local,
        mesh=fine,
        in_specs=(
            rows,
            P(ZAXES, None),
            P(ZAXES, None),
            P(experts, None, ZAXES),
            P(experts, None, ZAXES),
            P(experts, ZAXES, None),
            rows,
        ),
        out_specs=(rows, rows, rows),
        check_vma=False,
    )
```
